128 devices in a mesh: px: 8 (over x, core), py: 16 (over y, z).
Axes of the slice: x: 4, y: 4, z: 4, core: 2. Of those that a mesh axis runs over, the one named last changes fastest.
Arguments:
- modes_disp: bfloat16 [288, 262144], P(None, ('px', 'py')), may hold values from -6 to 6
- recovery: bfloat16 [24, 24, 262144], P(None, None, ('px', 'py')), may hold values from -1.25 to 1.25
- connect: int32 [4, 262144], P(None, ('px', 'py')), may hold values from 0 to 2047, as said below
- read_elem: int32 [65536], P(('px', 'py')), may hold values from 0 to 2047
- read_wts: float32 [24, 65536], P(None, ('px', 'py')), may hold values from -1.25 to 1.25
- zone: int32 [65536, 1], P(('px', 'py')), may hold values from 0 to 127; in each aligned block of 512 rows (0 to 511, 512 to 1023, ...) at most 8 rows name the same one
- response: bfloat16 [48, 576], replicated, may hold values from -0.875 to 0.875
Outputs:
- transfer: bfloat16 [131072, 576], P(('px', 'py'))
The draws below stay inside these ranges and needn't reach their ends.
Inputs may be any that keep to these rules, and one draw needn't show every extreme that they name: `connect`: each partition's 2048 columns name every one of its 2048 nodes at least once. Among the read-out points of one partition no zone is named more than 8 times, a bound that some block reaches.
All inputs are finite; a program needn't handle non-finite values.
Results may differ from the reference program's by a relative error of at most 0.005.
Values may be sent and summed in bfloat16 or wider, within the bound.
No kernel may reach another device: no remote copies, remote signals or barrier semaphores. Data moves between devices by JAX's collectives and lax.ppermute only.
A program may use at most 64 MiB of HBM per device.

```python
import math
import jax
import jax.numpy as jnp
import numpy as np
from jax import lax

MODES = 48
CORNERS = 4
DOFS = 6
COMPS = 6
ELEM_DEV = 2048
NODE_DEV = 2048
BORDER = 32
READ_DEV = 512
ZONES = 128
CAP = 8
READS = 65536
ELEMENTS = 262144
NODES = 262144
COLS = 576
N_PX = 8
N_PY = 16


def draw_connect(key, part):

    def one_block(subkey):
        first_key, second_key, third_key = jax.random.split(subkey, 3)
        covering = jax.random.permutation(first_key, NODE_DEV).astype(jnp.int32)
        further = jax.random.randint(second_key, (CORNERS * ELEM_DEV - NODE_DEV,), 0, NODE_DEV).astype(jnp.int32)
        mixed = jax.random.permutation(third_key, jnp.concatenate([covering, further]))
        return mixed.reshape(CORNERS, ELEM_DEV)
    block_keys = jax.random.split(jax.random.fold_in(key, 11), ZONES)
    blocks = jax.vmap(one_block)(block_keys)
    return jnp.transpose(blocks, (1, 0, 2)).reshape(CORNERS, ZONES * ELEM_DEV)


def set_ends(values, rng, low, largest):
    index_at = [jax.random.randint(jax.random.fold_in(rng, axis), (), 0, length) for axis, length in enumerate(values.shape)]
    main_axis = values.shape.index(max(values.shape))
    next_to = index_at[:main_axis] + [(index_at[main_axis] + 1) % values.shape[main_axis]] + index_at[main_axis + 1:]
    return values.at[tuple(index_at)].set(low).at[tuple(next_to)].set(largest)


def block_levels(stream_key, shape, cuts, smallest, top_value):
    factor_of = 1.0
    for axis_at, blocks in cuts:
        heights = jax.random.uniform(jax.random.fold_in(jax.random.fold_in(stream_key, 6), axis_at), (blocks,), jnp.float32, smallest / len(cuts), top_value / len(cuts))
        factor_of = factor_of * jnp.repeat(jnp.exp(heights), shape[axis_at] // blocks).reshape((-1,) + (1,) * (len(shape) - 1 - axis_at))
    return factor_of


def deal_out(rng, own, number, rows, count, top, reach, skew):
    order = jax.random.permutation(rng, count)
    crowded, ordinary = shares(count, rows * top, reach, skew, True), shares(count, rows * top, reach, skew, False)
    places = jnp.arange(count)

    def named(tallies, rotation):
        used = int((tallies > 0).sum())
        fixed = max(1, used // 4)
        moved = fixed + (places - fixed + rotation * (used - fixed)) % max(1, count - fixed)
        return jnp.zeros((count,), jnp.int32).at[order[jnp.where(places < fixed, places, moved)]].set(jnp.asarray(tallies, jnp.int32))

    tallies = jnp.where(number % 4 == 0, named(crowded, number // 4), named(ordinary, number - number // 4 - 1))
    mixed = jax.random.permutation(jax.random.fold_in(own, 3), count)
    donor, receiver = mixed[0:count // 2 * 2:2], mixed[1:count // 2 * 2:2]
    room = jnp.minimum(tallies[donor] - 1, reach - tallies[receiver]) // 2
    room = jnp.where((donor == order[0]) | (receiver == order[0]) | (tallies[receiver] == 0), 0, jnp.maximum(room, 0))
    moved = jax.random.randint(jax.random.fold_in(own, 4), (count // 2,), 0, 1 << 20) % (room + 1)
    tallies = tallies.at[donor].add(-moved).at[receiver].add(moved)
    items = jnp.searchsorted(jnp.cumsum(tallies), jnp.arange(rows * top), side="right").astype(jnp.int32)
    grid = items.reshape(top, rows).T
    grid = grid[jax.random.permutation(jax.random.fold_in(own, 1), rows)]
    rotation = jax.random.randint(jax.random.fold_in(own, 2), (rows, 1), 0, top)
    return jnp.take_along_axis(grid, (jnp.arange(top)[None, :] + rotation) % top, axis=1)


def shares(amount, total, reach, skew, full):
    portions = [(1 << 20) // math.isqrt(rank ** skew) + 1 for rank in range(1, amount + 1)]
    largest = reach if full else min(reach, max(-(-total // amount), total * portions[0] // sum(portions)))
    least = 1 if total - largest >= amount - 1 else 0
    holding, rest = [largest] + [least] * (amount - 1), total - largest - least * (amount - 1)
    while rest > 0:
        candidates = [i for i in range(1, amount) if holding[i] < largest] or [i for i in range(1, amount) if holding[i] < reach]
        mass, left = sum([portions[i] for i in candidates]), rest
        for i in candidates:
            more = min(reach - holding[i], max(1, left * portions[i] // mass), rest)
            holding[i] = holding[i] + more
            rest = rest - more
    return np.array(holding)


def centred(key, extent, width, limit, cuts=(), kind=jnp.bfloat16):
    drawn = jax.random.normal(key, extent, jnp.float32) * width
    if len(cuts) > 0:
        drawn = block_levels(key, extent, cuts, -0.22, 0.18) * drawn
    return jnp.clip(drawn, min=-limit, max=limit).astype(kind)


def setup_inputs(seed: int = 0) -> dict:
    arg_keys = jax.random.split(jax.random.key(seed), 8)
    modes_disp = centred(arg_keys[0], (DOFS * MODES, NODES), 1.0, 6.0, ((1, 128),))
    recovery = centred(arg_keys[1], (CORNERS * COMPS, CORNERS * DOFS, ELEMENTS), (CORNERS * DOFS) ** -0.5, 1.25, ((2, 128),))
    connect = draw_connect(jax.random.fold_in(arg_keys[7], 71), 0)
    read_elem = set_ends(jax.random.randint(arg_keys[3], (READS,), 0, ELEM_DEV), jax.random.fold_in(arg_keys[3], 1), 0, ELEM_DEV - 1).astype(jnp.int32)
    read_wts = centred(arg_keys[4], (CORNERS * COMPS, READS), (CORNERS * COMPS) ** -0.5, 1.25, ((1, 128),), jnp.float32)
    zone_keys = jax.random.split(jax.random.fold_in(arg_keys[5], 1), READS // READ_DEV)
    zone_turns = jax.random.permutation(jax.random.fold_in(arg_keys[5], 3), READS // READ_DEV)
    zone = jax.vmap(lambda own, number: deal_out(jax.random.fold_in(arg_keys[5], 2), own, number, READ_DEV, ZONES, 1, CAP, 2))(zone_keys, zone_turns).reshape((READS, 1))
    response = centred(arg_keys[6], (MODES, COLS), MODES ** -0.5, 0.875)
    return {"modes_disp": modes_disp, "recovery": recovery, "connect": connect, "read_elem": read_elem, "read_wts": read_wts, "zone": zone, "response": response}


def corner_stress(modes_block, recovery_block, connect_block):
    gathered = jnp.take(modes_block, connect_block, axis=1).astype(jnp.float32)
    gathered = gathered.reshape(DOFS, MODES, CORNERS, ELEM_DEV)
    matrices = recovery_block.astype(jnp.float32).reshape(CORNERS * COMPS, CORNERS, DOFS, ELEM_DEV)
    stress = jnp.einsum('rcde,dmce->rme', matrices, gathered, precision=lax.Precision.HIGHEST)
    stress = stress.reshape(CORNERS, COMPS * MODES, ELEM_DEV)
    partial_value = jnp.zeros((COMPS * MODES, NODE_DEV), jnp.float32)
    counts = jnp.zeros((NODE_DEV,), jnp.float32)
    for corner in range(CORNERS):
        partial_value = partial_value.at[:, connect_block[corner]].add(stress[corner])
        counts = counts.at[connect_block[corner]].add(1.0)
    return partial_value, counts


def readout(node_stress, connect_block, elements, weights):
    nodes = jnp.take(connect_block, elements, axis=1)
    picked = jnp.take(node_stress, nodes, axis=1).reshape(COMPS, MODES, CORNERS, -1)
    shaped = weights.reshape(CORNERS, COMPS, -1)
    return jnp.einsum('kmcr,ckr->rm', picked, shaped, precision=lax.Precision.HIGHEST).astype(jnp.bfloat16)


def from_lower(values, along):
    padding = [(0, 0)] * values.ndim
    padding[along] = (1, 0)
    return lax.slice_in_dim(jnp.pad(values, padding), 0, values.shape[along], axis=along)


def from_upper(values, along):
    padding = [(0, 0)] * values.ndim
    padding[along] = (0, 1)
    return lax.slice_in_dim(jnp.pad(values, padding), 1, values.shape[along] + 1, axis=along)


def side_totals(slab):
    west_side = slab[..., 0, :]
    east_side = slab[..., 1, :]
    south_side = slab[..., 2, :]
    north_side = slab[..., 3, :]
    new_west = west_side + from_lower(east_side, 0)
    new_east = east_side + from_upper(west_side, 0)
    new_south = south_side + from_lower(north_side, 1)
    new_north = north_side + from_upper(south_side, 1)
    return jnp.stack([new_west, new_east, new_south, new_north], axis=-2)


def rank_within(targets):
    onehot = (targets[:, None] == jnp.arange(ZONES)[None, :]).astype(jnp.int32)
    before = jnp.cumsum(onehot, axis=0) - onehot
    return jnp.sum(before * onehot, axis=1).astype(jnp.int32)


def reference(modes_disp, recovery, connect, read_elem, read_wts, zone, response):
    modes_blocks = modes_disp.reshape(DOFS * MODES, ZONES, NODE_DEV).transpose(1, 0, 2)
    recovery_blocks = recovery.reshape(CORNERS * COMPS, CORNERS * DOFS, ZONES, ELEM_DEV).transpose(2, 0, 1, 3)
    connect_blocks = connect.reshape(CORNERS, ZONES, ELEM_DEV).transpose(1, 0, 2)

    def borders(pieces):
        partial_value, counts = corner_stress(pieces[0], pieces[1], pieces[2])
        return partial_value[:, :4 * BORDER], counts[:4 * BORDER]

    slabs, slab_counts = lax.map(borders, (modes_blocks, recovery_blocks, connect_blocks))
    slabs = side_totals(slabs.reshape(N_PX, N_PY, COMPS * MODES, 4, BORDER)).reshape(ZONES, COMPS * MODES, 4 * BORDER)
    slab_counts = side_totals(slab_counts.reshape(N_PX, N_PY, 4, BORDER)).reshape(ZONES, 4 * BORDER)
    element_blocks = read_elem.reshape(ZONES, READ_DEV)
    weight_blocks = read_wts.reshape(CORNERS * COMPS, ZONES, READ_DEV).transpose(1, 0, 2)

    def hotspot(pieces):
        modes_block, recovery_block, connect_block, slab, slab_count, elements, weights = pieces
        partial_value, counts = corner_stress(modes_block, recovery_block, connect_block)
        partial_value = jnp.concatenate([slab, partial_value[:, 4 * BORDER:]], axis=1)
        counts = jnp.concatenate([slab_count, counts[4 * BORDER:]])
        node_stress = partial_value / counts[None, :]
        return readout(node_stress, connect_block, elements, weights)

    hot_rows = lax.map(hotspot, (modes_blocks, recovery_blocks, connect_blocks, slabs, slab_counts, element_blocks, weight_blocks))
    targets = zone.reshape(ZONES, READ_DEV)
    ranking = jax.vmap(rank_within)(targets)
    sources = jnp.arange(ZONES, dtype=jnp.int32)[:, None]
    rows_at = (targets * (ZONES * CAP) + sources * CAP + ranking).astype(jnp.int32)
    received = jnp.zeros((ZONES * ZONES * CAP, MODES), jnp.bfloat16)
    received = received.at[rows_at.reshape(-1)].set(hot_rows.reshape(-1, MODES))

    def product(block_rows):
        return jnp.dot(block_rows, response, preferred_element_type=jnp.float32).astype(jnp.bfloat16)

    result = lax.map(product, received.reshape(ZONES, ZONES * CAP, MODES))
    return result.reshape(ZONES * ZONES * CAP, COLS)
```

```python
import functools

import jax
import jax.numpy as jnp
from jax import lax
from jax.experimental import pallas as pl
from jax.experimental.pallas import tpu as pltpu
from jax.sharding import PartitionSpec as P

MODES = 48
CORNERS = 4
DOFS = 6
COMPS = 6
BORDER = 32
ROWS = COMPS * MODES
TALL = ROWS + 16
WIDE = 384
BLOCK = 256
TILE = 256
CHUNK = 512
LANES = 128
BF = jnp.bfloat16
F32 = jnp.float32


def hot(mask):
    return jnp.where(mask, jnp.ones((), BF), jnp.zeros((), BF))


def rows16(row):
    return jnp.broadcast_to(row, (16, row.shape[1])).astype(jnp.int16)


def tall16(row, count):
    width = row.shape[1]
    return jnp.broadcast_to(row[None], (count // 16, 16, width)).reshape(count, width)


def column_ids(connect_block):
    padded = jnp.concatenate([connect_block, connect_block], axis=0)
    turned = jnp.transpose(padded)
    parts = [
        jnp.broadcast_to(turned[:, c : c + 1], (BLOCK, LANES)).astype(jnp.int16)
        for c in range(CORNERS)
    ]
    return jnp.concatenate(parts, axis=0)


def stress_kernel(
    modes, recovery, connect, elems, acc, side_w, side_e, side_s, side_n, ids_out,
    rf, vn, vc, p_cur, p_prev, colb, qrow, accb,
):
    step = pl.program_id(0)
    steps = pl.num_programs(0)
    nodes = modes.shape[1]
    tiles = acc.shape[0]
    ones = jnp.ones((16, 2 * BLOCK), BF)

    def gather(corner, part, row):
        base = pl.multiple_of(part * CHUNK, CHUNK)
        ids = lax.broadcasted_iota(jnp.int16, (CHUNK, BLOCK), 0)
        mask = ids == tall16(rows16(row - base), CHUNK)
        return jnp.dot(modes[:, pl.ds(base, CHUNK)], hot(mask), preferred_element_type=F32)

    def scatter(tile, half):
        base = pl.multiple_of(half * 2 * BLOCK, 2 * BLOCK)
        lhs = jnp.concatenate(
            [
                p_prev[pl.ds(half * 2 * COMPS, COMPS)].reshape(ROWS, BLOCK),
                p_prev[pl.ds(half * 2 * COMPS + COMPS, COMPS)].reshape(ROWS, BLOCK),
            ],
            axis=1,
        )
        lhs = jnp.concatenate([lhs, ones], axis=0)
        ids = colb[pl.ds(base, 2 * BLOCK), :]
        mask = jnp.concatenate([ids, ids], axis=1) == tall16(qrow[tile], 2 * BLOCK)
        return jnp.dot(lhs, hot(mask), preferred_element_type=F32)

    @pl.when(step == 0)
    def _():
        ids = connect[...]
        high = lax.shift_right_logical(ids, 4)
        low = ids - high * 16
        split = jnp.concatenate([high, low], axis=0).astype(F32)
        split = jnp.concatenate([split, jnp.zeros_like(split)], axis=0).astype(BF)
        reads = elems.shape[1]
        got = jnp.zeros((16, reads), F32)
        for part in range(nodes // CHUNK):
            iota = lax.broadcasted_iota(jnp.int16, (CHUNK, reads), 0)
            mask = iota == tall16(rows16(elems[...] - part * CHUNK), CHUNK)
            got = got + jnp.dot(split[:, part * CHUNK : (part + 1) * CHUNK], hot(mask), preferred_element_type=F32)
        found = (got[0:4] * 16.0 + got[4:8]).astype(jnp.int32)
        ids_out[...] = found
        for tile in range(tiles):
            c, part = tile // (reads // TILE), tile % (reads // TILE)
            qrow[tile] = rows16(found[c : c + 1, part * TILE : (part + 1) * TILE])
        acc[...] = jnp.zeros_like(acc)
        accb[...] = jnp.zeros_like(accb)
        p_prev[...] = jnp.zeros_like(p_prev)
        colb[...] = jnp.full(colb.shape, -1, jnp.int16)

        for corner in range(CORNERS):
            row = connect[corner : corner + 1, 0:BLOCK]
            total = gather(corner, 0, row)
            for part in range(1, nodes // CHUNK):
                total = total + gather(corner, part, row)
            vc[corner] = total

    @pl.when(step > 0)
    def _():
        vc[...] = vn[...]

    vn[...] = jnp.zeros_like(vn)
    rf[...] = recovery[...].astype(F32)
    after = pl.multiple_of(jnp.minimum(step + 1, steps - 1) * BLOCK, BLOCK)

    @pl.loop(0, 16)
    def _(t):
        corner, part = t // 4, t % 4
        row = connect[pl.ds(corner, 1), pl.ds(after, BLOCK)]
        vn[corner] += gather(corner, part, row)
        acc[t % 8] += scatter(t % 8, t // 8)
        lanes = pl.ds(pl.multiple_of((t // 8) * LANES, LANES), LANES)
        first = (t % 8) * 3
        sums = [None] * 3
        for j in range(CORNERS * DOFS):
            moved = vc[j // DOFS, (j % DOFS) * MODES : (j % DOFS + 1) * MODES, lanes]
            for q in range(3):
                term = rf[first + q, j : j + 1, lanes] * moved
                sums[q] = term if j == 0 else sums[q] + term
        for q in range(3):
            p_cur[first + q, :, lanes] = sums[q].astype(BF)

    now = pl.multiple_of(step * BLOCK, BLOCK)
    p_prev[...] = p_cur[...]
    colb[...] = column_ids(connect[:, pl.ds(now, BLOCK)])
    lane_ids = lax.broadcasted_iota(jnp.int16, (2 * BLOCK, LANES), 1)
    for half in range(2):
        lhs = jnp.concatenate(
            [
                p_cur[half * 2 * COMPS + c * COMPS : half * 2 * COMPS + (c + 1) * COMPS].reshape(ROWS, BLOCK)
                for c in range(2)
            ],
            axis=1,
        )
        lhs = jnp.concatenate([lhs, ones], axis=0)
        mask = colb[half * 2 * BLOCK : (half + 1) * 2 * BLOCK, :] == lane_ids
        accb[...] += jnp.dot(lhs, hot(mask), preferred_element_type=F32)

    @pl.when(step == steps - 1)
    def _():
        tall = jnp.concatenate([accb[...], jnp.zeros((WIDE - TALL, LANES), F32)], axis=0)
        turned = jnp.transpose(tall)
        count = turned[:, ROWS : ROWS + 1].astype(jnp.int32)
        high = lax.shift_right_logical(count, 7)
        low = (count - high * 128).astype(F32)
        high = high.astype(F32)
        lane = lax.broadcasted_iota(jnp.int32, (LANES, WIDE), 1)
        out = jnp.where(lane < ROWS, turned, 0.0)
        out = jnp.where(lane == ROWS, high, out)
        out = jnp.where(lane == ROWS + 1, low, out).astype(BF)
        for side, ref in enumerate((side_w, side_e, side_s, side_n)):
            ref[...] = out[side * BORDER : (side + 1) * BORDER, :]

        @pl.loop(0, 16)
        def _(t):
            acc[t % 8] += scatter(t % 8, t // 8)


def readout_kernel(flags, acc, ids, got_w, got_e, got_s, got_n, weights, zone, out, *, zones, cap):
    reads = ids.shape[1]
    halves = reads // TILE
    pieces = []
    for side, ref in enumerate((got_w, got_e, got_s, got_n)):
        value = ref[...].astype(F32)
        pieces.append(jnp.where(flags[side] > 0, value, jnp.zeros_like(value)))
    border = jnp.transpose(jnp.concatenate(pieces, axis=0)).astype(BF)
    spots = [jnp.zeros((MODES, TILE), F32) for _ in range(halves)]
    iota = lax.broadcasted_iota(jnp.int32, (4 * BORDER, TILE), 0)
    for tile in range(acc.shape[0]):
        c, part = tile // halves, tile % halves
        at = slice(part * TILE, (part + 1) * TILE)
        mask = iota == ids[c : c + 1, at]
        more = jnp.dot(border, mask.astype(F32).astype(BF), preferred_element_type=F32)
        count = acc[tile, ROWS : ROWS + 1, :] + (more[ROWS : ROWS + 1] * 128.0 + more[ROWS + 1 : ROWS + 2])
        share = weights[c * COMPS : (c + 1) * COMPS, at] / count
        for k in range(COMPS):
            rows = slice(k * MODES, (k + 1) * MODES)
            spots[part] = spots[part] + share[k : k + 1] * (acc[tile, rows, :] + more[rows])
    spot = jnp.concatenate(spots, axis=1)
    spot = jnp.concatenate([spot, jnp.zeros((LANES - MODES, reads), F32)], axis=0)
    spot = jnp.transpose(spot).astype(BF)
    row = zone[...]
    column = jnp.transpose(jnp.broadcast_to(row, (8, reads)))[:, 0:1]
    at_row = lax.broadcasted_iota(jnp.int32, (reads, reads), 1)
    at_col = lax.broadcasted_iota(jnp.int32, (reads, reads), 0)
    same = jnp.where((column == row) & (at_col < at_row), 1.0, 0.0)
    rank = jnp.sum(same, axis=0, keepdims=True).astype(jnp.int32)
    slot = row * cap + rank
    chunk = 256
    for base in range(0, zones * cap, chunk):
        chosen = lax.broadcasted_iota(jnp.int32, (chunk, reads), 0) + base == slot
        out[base : base + chunk, :] = jnp.dot(
            chosen.astype(F32).astype(BF), spot, preferred_element_type=F32
        ).astype(BF)


def response_kernel(rows, response, out):
    out[...] = jnp.dot(rows[:, :MODES], response[...], preferred_element_type=F32).astype(BF)


def ring(x, axis, by):
    count = lax.axis_size(axis)
    return lax.ppermute(x, axis, [(i, (i + by) % count) for i in range(count)])


def params():
    return pltpu.CompilerParams(vmem_limit_bytes=56 * 2**20)


def per_device(modes_disp, recovery, connect, read_elem, read_wts, zone, response):
    elements = connect.shape[1]
    nodes = modes_disp.shape[1]
    reads = read_elem.shape[0]
    px, py = lax.axis_size("px"), lax.axis_size("py")
    zones = px * py
    cap = max(2, 2 * reads // zones)
    tiles = CORNERS * reads // TILE
    full = pl.BlockSpec(memory_space=pltpu.VMEM)
    side = jax.ShapeDtypeStruct((BORDER, WIDE), BF)
    whole = lambda *shape: pl.BlockSpec(shape, lambda i: (0,) * len(shape))
    acc, part_w, part_e, part_s, part_n, ids = pl.pallas_call(
        stress_kernel,
        grid=(elements // BLOCK,),
        in_specs=[
            whole(ROWS, nodes),
            pl.BlockSpec((CORNERS * COMPS, CORNERS * DOFS, BLOCK), lambda i: (0, 0, i)),
            whole(CORNERS, elements),
            whole(1, reads),
        ],
        out_specs=[whole(tiles, TALL, TILE)] + [whole(BORDER, WIDE)] * 4 + [whole(CORNERS, reads)],
        out_shape=[
            jax.ShapeDtypeStruct((tiles, TALL, TILE), F32),
            side, side, side, side,
            jax.ShapeDtypeStruct((CORNERS, reads), jnp.int32),
        ],
        scratch_shapes=[
            pltpu.VMEM((CORNERS * COMPS, CORNERS * DOFS, BLOCK), F32),
            pltpu.VMEM((CORNERS, ROWS, BLOCK), F32),
            pltpu.VMEM((CORNERS, ROWS, BLOCK), F32),
            pltpu.VMEM((CORNERS * COMPS, MODES, BLOCK), BF),
            pltpu.VMEM((CORNERS * COMPS, MODES, BLOCK), BF),
            pltpu.VMEM((CORNERS * BLOCK, LANES), jnp.int16),
            pltpu.VMEM((tiles, 16, TILE), jnp.int16),
            pltpu.VMEM((TALL, LANES), F32),
        ],
        compiler_params=params(),
        name="stress",
    )(modes_disp, recovery, connect, read_elem.reshape(1, reads))
    got_w = ring(part_e, "px", 1)
    got_e = ring(part_w, "px", -1)
    got_s = ring(part_n, "py", 1)
    got_n = ring(part_s, "py", -1)
    i, j = lax.axis_index("px"), lax.axis_index("py")
    flags = jnp.stack([i > 0, i < px - 1, j > 0, j < py - 1]).astype(jnp.int32)
    outgoing = pl.pallas_call(
        functools.partial(readout_kernel, zones=zones, cap=cap),
        in_specs=[pl.BlockSpec(memory_space=pltpu.SMEM)] + [full] * 8,
        out_specs=full,
        out_shape=jax.ShapeDtypeStruct((zones * cap, LANES), BF),
        compiler_params=params(),
        name="readout",
    )(flags, acc, ids, got_w, got_e, got_s, got_n, read_wts, zone.reshape(1, reads))
    arrived = lax.all_to_all(
        outgoing.reshape(zones, cap, LANES), ("px", "py"), split_axis=0, concat_axis=0, tiled=True
    ).reshape(zones * cap, LANES)
    cols = response.shape[1]
    split = 4
    return pl.pallas_call(
        response_kernel,
        grid=(split,),
        in_specs=[pl.BlockSpec((zones * cap // split, LANES), lambda i: (i, 0)), whole(MODES, cols)],
        out_specs=pl.BlockSpec((zones * cap // split, cols), lambda i: (i, 0)),
        out_shape=jax.ShapeDtypeStruct((zones * cap, cols), BF),
        compiler_params=params(),
        name="transfer",
    )(arrived, response)


def solution(mesh):
    placed = (
        P(None, ("px", "py")),
        P(None, None, ("px", "py")),
        P(None, ("px", "py")),
        P(("px", "py")),
        P(None, ("px", "py")),
        P(("px", "py"), None),
        P(),
    )
    return jax.shard_map(
        per_device, mesh=mesh, in_specs=placed, out_specs=P(("px", "py"), None), check_vma=False
    )
```

```python
import functools

import jax
import jax.numpy as jnp
from jax import lax
from jax.experimental import pallas as pl
from jax.experimental.pallas import tpu as pltpu
from jax.sharding import PartitionSpec as P

MODES = 48
CORNERS = 4
DOFS = 6
COMPS = 6
BORDER = 32
ROWS = COMPS * MODES
TALL = ROWS + 16
WIDE = 384
BLOCK = 256
TILE = 256
GROUP = 12
STRIP = 16
LANES = 128
BF = jnp.bfloat16
F32 = jnp.float32


def hot(mask):
    return jnp.where(mask, jnp.ones((), BF), jnp.zeros((), BF))


def rows16(row):
    return jnp.broadcast_to(row, (16, row.shape[1])).astype(jnp.int16)


def tall16(row, count):
    width = row.shape[1]
    return jnp.broadcast_to(row[None], (count // 16, 16, width)).reshape(count, width)


def column_ids(connect_block):
    count = connect_block.shape[1]
    padded = jnp.concatenate([connect_block, connect_block], axis=0)
    turned = jnp.transpose(padded)
    parts = [
        jnp.broadcast_to(turned[:, c : c + 1], (count, LANES)).astype(jnp.int16)
        for c in range(CORNERS)
    ]
    return jnp.concatenate(parts, axis=0)


def with_ones(stress):
    count = stress.shape[2]
    sides = [stress[c * COMPS : (c + 1) * COMPS].reshape(ROWS, count) for c in range(CORNERS)]
    return jnp.concatenate(
        [jnp.concatenate(sides, axis=1), jnp.ones((TALL - ROWS, CORNERS * count), BF)], axis=0
    )


def stress_kernel(modes, recovery, connect, stress, side_w, side_e, side_s, side_n, rf, vc, accb):
    step = pl.program_id(0)
    nodes = modes.shape[1]

    @pl.when(step == 0)
    def _():
        accb[...] = jnp.zeros_like(accb)

    rf[...] = recovery[...].astype(F32)
    for corner in range(CORNERS):
        row = tall16(rows16(connect[corner : corner + 1, :]), nodes)
        ids = lax.broadcasted_iota(jnp.int16, (nodes, BLOCK), 0)
        vc[corner] = jnp.dot(modes[...], hot(ids == row), preferred_element_type=F32)

    for half in range(BLOCK // LANES):
        lanes = slice(half * LANES, (half + 1) * LANES)

        @pl.loop(0, CORNERS * COMPS // GROUP)
        def _(t):
            first = t * GROUP
            for part in range(MODES // STRIP):
                sums = [None] * GROUP
                for j in range(CORNERS * DOFS):
                    base = (j % DOFS) * MODES + part * STRIP
                    moved = vc[j // DOFS, base : base + STRIP, lanes]
                    for q in range(GROUP):
                        term = rf[first + q, j : j + 1, lanes] * moved
                        sums[q] = term if j == 0 else sums[q] + term
                for q in range(GROUP):
                    stress[first + q, part * STRIP : (part + 1) * STRIP, lanes] = sums[q].astype(BF)

    lane_ids = lax.broadcasted_iota(jnp.int16, (CORNERS * BLOCK, LANES), 1)
    mask = column_ids(connect[...]) == lane_ids
    accb[...] += jnp.dot(with_ones(stress[...]), hot(mask), preferred_element_type=F32)

    @pl.when(step == pl.num_programs(0) - 1)
    def _():
        tall = jnp.concatenate([accb[...], jnp.zeros((WIDE - TALL, LANES), F32)], axis=0)
        turned = jnp.transpose(tall)
        count = turned[:, ROWS : ROWS + 1].astype(jnp.int32)
        high = lax.shift_right_logical(count, 7)
        low = (count - high * 128).astype(F32)
        high = high.astype(F32)
        lane = lax.broadcasted_iota(jnp.int32, (LANES, WIDE), 1)
        out = jnp.where(lane < ROWS, turned, 0.0)
        out = jnp.where(lane == ROWS, high, out)
        out = jnp.where(lane == ROWS + 1, low, out).astype(BF)
        for side, ref in enumerate((side_w, side_e, side_s, side_n)):
            ref[...] = out[side * BORDER : (side + 1) * BORDER, :]


def weighted(values, shares, c, at):
    total = None
    for k in range(COMPS):
        term = shares[c * COMPS + k : c * COMPS + k + 1, at] * values[k * MODES : (k + 1) * MODES]
        total = term if k == 0 else total + term
    return total


def scatter_kernel(stress, connect, whole, elems, weights, spots, ids_out, colb, qrow, acc):
    step = pl.program_id(0)
    tiles = acc.shape[0]
    nodes = whole.shape[1]
    reads = elems.shape[1]
    halves = reads // TILE

    @pl.when(step == 0)
    def _():
        ids = whole[...]
        high = lax.shift_right_logical(ids, 4)
        low = ids - high * 16
        split = jnp.concatenate([high, low], axis=0).astype(F32)
        split = jnp.concatenate([split, jnp.zeros_like(split)], axis=0).astype(BF)
        iota = lax.broadcasted_iota(jnp.int16, (nodes, reads), 0)
        mask = iota == tall16(rows16(elems[...]), nodes)
        got = jnp.dot(split, hot(mask), preferred_element_type=F32)
        found = (got[0:4] * 16.0 + got[4:8]).astype(jnp.int32)
        ids_out[...] = found
        for tile in range(tiles):
            c, part = tile // halves, tile % halves
            qrow[tile] = rows16(found[c : c + 1, part * TILE : (part + 1) * TILE])
        acc[...] = jnp.zeros_like(acc)

    colb[...] = column_ids(connect[...])

    @pl.loop(0, tiles // 2)
    def _(t):
        lhs = with_ones(stress[...])
        ids = jnp.concatenate([colb[...], colb[...]], axis=1)
        for u in range(2):
            mask = ids == tall16(qrow[t * 2 + u], colb.shape[0])
            acc[t * 2 + u] += jnp.dot(lhs, hot(mask), preferred_element_type=F32)

    @pl.when(step == pl.num_programs(0) - 1)
    def _():
        for tile in range(tiles):
            c, part = tile // halves, tile % halves
            at = slice(part * TILE, (part + 1) * TILE)
            spots[c, 0:MODES, at] = weighted(acc[tile, 0:ROWS, :], weights, c, at)
            spots[c, MODES : MODES + 8, at] = acc[tile, ROWS : ROWS + 8, :]


def readout_kernel(flags, near, ids, got_w, got_e, got_s, got_n, weights, zone, out, *, zones, cap):
    reads = ids.shape[1]
    halves = reads // TILE
    pieces = []
    for side, ref in enumerate((got_w, got_e, got_s, got_n)):
        value = ref[...].astype(F32)
        pieces.append(jnp.where(flags[side] > 0, value, jnp.zeros_like(value)))
    border = jnp.transpose(jnp.concatenate(pieces, axis=0))[0:TALL].astype(BF)
    spots = [None] * halves
    iota = lax.broadcasted_iota(jnp.int32, (4 * BORDER, TILE), 0)
    for part in range(halves):
        at = slice(part * TILE, (part + 1) * TILE)
        for c in range(CORNERS):
            mask = iota == ids[c : c + 1, at]
            more = jnp.dot(border, mask.astype(F32).astype(BF), preferred_element_type=F32)
            count = near[c, MODES : MODES + 1, at] + (
                more[ROWS : ROWS + 1] * 128.0 + more[ROWS + 1 : ROWS + 2]
            )
            term = (near[c, 0:MODES, at] + weighted(more, weights, c, at)) / count
            spots[part] = term if c == 0 else spots[part] + term
    spot = jnp.concatenate(spots, axis=1)
    spot = jnp.concatenate([spot, jnp.zeros((LANES - MODES, reads), F32)], axis=0)
    spot = jnp.transpose(spot).astype(BF)
    row = zone[...]
    column = jnp.transpose(jnp.broadcast_to(row, (8, reads)))[:, 0:1]
    at_row = lax.broadcasted_iota(jnp.int32, (reads, reads), 1)
    at_col = lax.broadcasted_iota(jnp.int32, (reads, reads), 0)
    same = jnp.where((column == row) & (at_col < at_row), 1.0, 0.0)
    rank = jnp.sum(same, axis=0, keepdims=True).astype(jnp.int32)
    slot = row * cap + rank
    chunk = 256
    for base in range(0, zones * cap, chunk):
        chosen = lax.broadcasted_iota(jnp.int32, (chunk, reads), 0) + base == slot
        out[base : base + chunk, :] = jnp.dot(
            chosen.astype(F32).astype(BF), spot, preferred_element_type=F32
        ).astype(BF)


def response_kernel(rows, response, out):
    out[...] = lax.dot_general(
        response[...], rows[:, 0:MODES], (((0,), (1,)), ((), ())), preferred_element_type=F32
    ).astype(BF)


def ring(x, axis, by):
    count = lax.axis_size(axis)
    return lax.ppermute(x, axis, [(i, (i + by) % count) for i in range(count)])


def params():
    return pltpu.CompilerParams(vmem_limit_bytes=56 * 2**20)


def per_device(modes_disp, recovery, connect, read_elem, read_wts, zone, response):
    elements = connect.shape[1]
    nodes = modes_disp.shape[1]
    reads = read_elem.shape[0]
    px, py = lax.axis_size("px"), lax.axis_size("py")
    zones = px * py
    cap = max(2, 2 * reads // zones)
    tiles = CORNERS * reads // TILE
    full = pl.BlockSpec(memory_space=pltpu.VMEM)
    side = jax.ShapeDtypeStruct((BORDER, WIDE), BF)
    whole = lambda *shape: pl.BlockSpec(shape, lambda i: (0,) * len(shape))
    stress, part_w, part_e, part_s, part_n = pl.pallas_call(
        stress_kernel,
        grid=(elements // BLOCK,),
        in_specs=[
            whole(ROWS, nodes),
            pl.BlockSpec((CORNERS * COMPS, CORNERS * DOFS, BLOCK), lambda i: (0, 0, i)),
            pl.BlockSpec((CORNERS, BLOCK), lambda i: (0, i)),
        ],
        out_specs=[pl.BlockSpec((CORNERS * COMPS, MODES, BLOCK), lambda i: (0, 0, i))]
        + [whole(BORDER, WIDE)] * 4,
        out_shape=[
            jax.ShapeDtypeStruct((CORNERS * COMPS, MODES, elements), BF),
            side, side, side, side,
        ],
        scratch_shapes=[
            pltpu.VMEM((CORNERS * COMPS, CORNERS * DOFS, BLOCK), F32),
            pltpu.VMEM((CORNERS, ROWS, BLOCK), F32),
            pltpu.VMEM((TALL, LANES), F32),
        ],
        compiler_params=params(),
        cost_estimate=pl.CostEstimate(flops=10**10, bytes_accessed=10**7, transcendentals=0),
        name="stress",
    )(modes_disp, recovery, connect)
    got_w = ring(part_e, "px", 1)
    got_e = ring(part_w, "px", -1)
    got_s = ring(part_n, "py", 1)
    got_n = ring(part_s, "py", -1)
    big = 2 * BLOCK
    near, ids = pl.pallas_call(
        scatter_kernel,
        grid=(elements // big,),
        in_specs=[
            pl.BlockSpec((CORNERS * COMPS, MODES, big), lambda i: (0, 0, i)),
            pl.BlockSpec((CORNERS, big), lambda i: (0, i)),
            whole(CORNERS, elements),
            whole(1, reads),
            whole(CORNERS * COMPS, reads),
        ],
        out_specs=[whole(CORNERS, MODES + 8, reads), whole(CORNERS, reads)],
        out_shape=[
            jax.ShapeDtypeStruct((CORNERS, MODES + 8, reads), F32),
            jax.ShapeDtypeStruct((CORNERS, reads), jnp.int32),
        ],
        scratch_shapes=[
            pltpu.VMEM((CORNERS * big, LANES), jnp.int16),
            pltpu.VMEM((tiles, 16, TILE), jnp.int16),
            pltpu.VMEM((tiles, TALL, TILE), F32),
        ],
        compiler_params=params(),
        cost_estimate=pl.CostEstimate(flops=10**10, bytes_accessed=10**7, transcendentals=0),
        name="scatter",
    )(stress, connect, connect, read_elem.reshape(1, reads), read_wts)
    i, j = lax.axis_index("px"), lax.axis_index("py")
    flags = jnp.stack([i > 0, i < px - 1, j > 0, j < py - 1]).astype(jnp.int32)
    outgoing = pl.pallas_call(
        functools.partial(readout_kernel, zones=zones, cap=cap),
        in_specs=[pl.BlockSpec(memory_space=pltpu.SMEM)] + [full] * 8,
        out_specs=full,
        out_shape=jax.ShapeDtypeStruct((zones * cap, LANES), BF),
        compiler_params=params(),
        name="readout",
    )(flags, near, ids, got_w, got_e, got_s, got_n, read_wts, zone.reshape(1, reads))
    arrived = lax.all_to_all(
        outgoing.reshape(zones, cap, LANES), ("px", "py"), split_axis=0, concat_axis=0, tiled=True
    ).reshape(zones * cap, LANES)
    cols = response.shape[1]
    split = 4
    turned = pl.pallas_call(
        response_kernel,
        grid=(split,),
        in_specs=[pl.BlockSpec((zones * cap // split, LANES), lambda i: (i, 0)), whole(MODES, cols)],
        out_specs=pl.BlockSpec((cols, zones * cap // split), lambda i: (0, i)),
        out_shape=jax.ShapeDtypeStruct((cols, zones * cap), BF),
        compiler_params=params(),
        name="transfer",
    )(arrived, response)
    return jnp.transpose(turned)


def solution(mesh):
    placed = (
        P(None, ("px", "py")),
        P(None, None, ("px", "py")),
        P(None, ("px", "py")),
        P(("px", "py")),
        P(None, ("px", "py")),
        P(("px", "py"), None),
        P(),
    )
    return jax.shard_map(
        per_device, mesh=mesh, in_specs=placed, out_specs=P(("px", "py"), None), check_vma=False
    )
```

```python
import functools

import jax
import jax.numpy as jnp
from jax import lax
from jax.experimental import pallas as pl
from jax.experimental.pallas import tpu as pltpu
from jax.sharding import PartitionSpec as P

MODES = 48
CORNERS = 4
DOFS = 6
COMPS = 6
BORDER = 32
ROWS = COMPS * MODES
TALL = ROWS + 16
WIDE = 384
BLOCK = 256
TILE = 256
GROUP = 12
STRIP = 16
UNROLL = 2
LANES = 128
BF = jnp.bfloat16
F32 = jnp.float32


def hot(mask):
    return jnp.where(mask, jnp.ones((), BF), jnp.zeros((), BF))


def rows16(row):
    return jnp.broadcast_to(row, (16, row.shape[1])).astype(jnp.int16)


def tall16(row, count):
    width = row.shape[1]
    return jnp.broadcast_to(row[None], (count // 16, 16, width)).reshape(count, width)


def line16(connect):
    return jnp.concatenate([rows16(connect[c : c + 1, :]) for c in range(CORNERS)], axis=1)


def dot_rows(x, y):
    return lax.dot_general(x, y, (((1,), (1,)), ((), ())), preferred_element_type=F32)


def with_ones(stress):
    count = stress.shape[2]
    sides = [stress[c * COMPS : (c + 1) * COMPS].reshape(ROWS, count) for c in range(CORNERS)]
    return jnp.concatenate(
        [jnp.concatenate(sides, axis=1), jnp.ones((TALL - ROWS, CORNERS * count), BF)], axis=0
    )


def stress_kernel(modes, recovery, connect, stress, side_w, side_e, side_s, side_n, rf, vc, accb):
    step = pl.program_id(0)
    nodes = modes.shape[1]

    @pl.when(step == 0)
    def _():
        accb[...] = jnp.zeros_like(accb)

    rf[...] = recovery[...].astype(F32)
    for corner in range(CORNERS):
        row = tall16(rows16(connect[corner : corner + 1, :]), nodes)
        ids = lax.broadcasted_iota(jnp.int16, (nodes, BLOCK), 0)
        vc[corner] = jnp.dot(modes[...], hot(ids == row), preferred_element_type=F32)

    for half in range(BLOCK // LANES):
        lanes = slice(half * LANES, (half + 1) * LANES)

        @pl.loop(0, CORNERS * COMPS // GROUP)
        def _(t):
            first = t * GROUP
            for part in range(MODES // STRIP):
                sums = [None] * GROUP
                for j in range(CORNERS * DOFS):
                    base = (j % DOFS) * MODES + part * STRIP
                    moved = vc[j // DOFS, base : base + STRIP, lanes]
                    for q in range(GROUP):
                        term = rf[first + q, j : j + 1, lanes] * moved
                        sums[q] = term if j == 0 else sums[q] + term
                for q in range(GROUP):
                    stress[first + q, part * STRIP : (part + 1) * STRIP, lanes] = sums[q].astype(BF)

    ids = lax.broadcasted_iota(jnp.int16, (LANES, CORNERS * BLOCK), 0)
    accb[...] += dot_rows(with_ones(stress[...]), hot(ids == tall16(line16(connect), LANES)))

    @pl.when(step == pl.num_programs(0) - 1)
    def _():
        tall = jnp.concatenate([accb[...], jnp.zeros((WIDE - TALL, LANES), F32)], axis=0)
        turned = jnp.transpose(tall)
        count = turned[:, ROWS : ROWS + 1].astype(jnp.int32)
        high = lax.shift_right_logical(count, 7)
        low = (count - high * 128).astype(F32)
        high = high.astype(F32)
        lane = lax.broadcasted_iota(jnp.int32, (LANES, WIDE), 1)
        out = jnp.where(lane < ROWS, turned, 0.0)
        out = jnp.where(lane == ROWS, high, out)
        out = jnp.where(lane == ROWS + 1, low, out).astype(BF)
        for side, ref in enumerate((side_w, side_e, side_s, side_n)):
            ref[...] = out[side * BORDER : (side + 1) * BORDER, :]


def weighted(values, shares, c, at):
    total = None
    for k in range(COMPS):
        term = shares[c * COMPS + k : c * COMPS + k + 1, at] * values[k * MODES : (k + 1) * MODES]
        total = term if k == 0 else total + term
    return total


def scatter_kernel(stress, connect, whole, elems, weights, spots, ids_out, qcol, acc):
    step = pl.program_id(0)
    tiles = acc.shape[0]
    nodes = whole.shape[1]
    reads = elems.shape[1]
    halves = reads // TILE

    @pl.when(step == 0)
    def _():
        ids = whole[...]
        high = lax.shift_right_logical(ids, 4)
        low = ids - high * 16
        split = jnp.concatenate([high, low], axis=0).astype(F32)
        split = jnp.concatenate([split, jnp.zeros_like(split)], axis=0).astype(BF)
        iota = lax.broadcasted_iota(jnp.int16, (nodes, reads), 0)
        mask = iota == tall16(rows16(elems[...]), nodes)
        got = jnp.dot(split, hot(mask), preferred_element_type=F32)
        found = (got[0:4] * 16.0 + got[4:8]).astype(jnp.int32)
        ids_out[...] = found
        turned = jnp.transpose(jnp.concatenate([found, found], axis=0))
        for tile in range(tiles):
            c, part = tile // halves, tile % halves
            column = turned[part * TILE : (part + 1) * TILE, c : c + 1]
            qcol[tile] = jnp.broadcast_to(column, (TILE, LANES)).astype(jnp.int16)
        acc[...] = jnp.zeros_like(acc)

    @pl.loop(0, tiles // UNROLL)
    def _(t):
        lhs = with_ones(stress[...])
        line = tall16(line16(connect), TILE)
        for u in range(UNROLL):
            ids = qcol[t * UNROLL + u]
            mask = jnp.concatenate([ids] * (line.shape[1] // LANES), axis=1) == line
            acc[t * UNROLL + u] += dot_rows(lhs, hot(mask))

    @pl.when(step == pl.num_programs(0) - 1)
    def _():
        for tile in range(tiles):
            c, part = tile // halves, tile % halves
            at = slice(part * TILE, (part + 1) * TILE)
            spots[c, 0:MODES, at] = weighted(acc[tile, 0:ROWS, :], weights, c, at)
            spots[c, MODES : MODES + 8, at] = acc[tile, ROWS : ROWS + 8, :]


def readout_kernel(near, ids, got_w, got_e, got_s, got_n, weights, zone, out, *, zones, cap):
    reads = ids.shape[1]
    halves = reads // TILE
    i, j = lax.axis_index("px"), lax.axis_index("py")
    flags = (i > 0, i < lax.axis_size("px") - 1, j > 0, j < lax.axis_size("py") - 1)
    pieces = []
    for side, ref in enumerate((got_w, got_e, got_s, got_n)):
        value = ref[...].astype(F32)
        pieces.append(jnp.where(flags[side], value, jnp.zeros_like(value)))
    border = jnp.transpose(jnp.concatenate(pieces, axis=0))[0:TALL].astype(BF)
    spots = [None] * halves
    iota = lax.broadcasted_iota(jnp.int32, (4 * BORDER, TILE), 0)
    for part in range(halves):
        at = slice(part * TILE, (part + 1) * TILE)
        for c in range(CORNERS):
            mask = iota == ids[c : c + 1, at]
            more = jnp.dot(border, mask.astype(F32).astype(BF), preferred_element_type=F32)
            count = near[c, MODES : MODES + 1, at] + (
                more[ROWS : ROWS + 1] * 128.0 + more[ROWS + 1 : ROWS + 2]
            )
            term = (near[c, 0:MODES, at] + weighted(more, weights, c, at)) / count
            spots[part] = term if c == 0 else spots[part] + term
    spot = jnp.concatenate(spots, axis=1)
    spot = jnp.concatenate([spot, jnp.zeros((LANES - MODES, reads), F32)], axis=0)
    spot = jnp.transpose(spot).astype(BF)
    row = zone[...]
    column = jnp.transpose(jnp.broadcast_to(row, (8, reads)))[:, 0:1]
    at_row = lax.broadcasted_iota(jnp.int32, (reads, reads), 1)
    at_col = lax.broadcasted_iota(jnp.int32, (reads, reads), 0)
    same = jnp.where((column == row) & (at_col < at_row), 1.0, 0.0)
    rank = jnp.sum(same, axis=0, keepdims=True).astype(jnp.int32)
    slot = row * cap + rank
    chunk = 256
    for base in range(0, zones * cap, chunk):
        chosen = lax.broadcasted_iota(jnp.int32, (chunk, reads), 0) + base == slot
        out[base : base + chunk, :] = jnp.dot(
            chosen.astype(F32).astype(BF), spot, preferred_element_type=F32
        ).astype(BF)


def ring(x, axis, by):
    count = lax.axis_size(axis)
    return lax.ppermute(x, axis, [(i, (i + by) % count) for i in range(count)])


def params():
    return pltpu.CompilerParams(vmem_limit_bytes=56 * 2**20)


def per_device(modes_disp, recovery, connect, read_elem, read_wts, zone, response):
    elements = connect.shape[1]
    nodes = modes_disp.shape[1]
    reads = read_elem.shape[0]
    px, py = lax.axis_size("px"), lax.axis_size("py")
    zones = px * py
    cap = max(2, 2 * reads // zones)
    tiles = CORNERS * reads // TILE
    full = pl.BlockSpec(memory_space=pltpu.VMEM)
    side = jax.ShapeDtypeStruct((BORDER, WIDE), BF)
    whole = lambda *shape: pl.BlockSpec(shape, lambda i: (0,) * len(shape))
    stress, part_w, part_e, part_s, part_n = pl.pallas_call(
        stress_kernel,
        grid=(elements // BLOCK,),
        in_specs=[
            whole(ROWS, nodes),
            pl.BlockSpec((CORNERS * COMPS, CORNERS * DOFS, BLOCK), lambda i: (0, 0, i)),
            pl.BlockSpec((CORNERS, BLOCK), lambda i: (0, i)),
        ],
        out_specs=[pl.BlockSpec((CORNERS * COMPS, MODES, BLOCK), lambda i: (0, 0, i))]
        + [whole(BORDER, WIDE)] * 4,
        out_shape=[
            jax.ShapeDtypeStruct((CORNERS * COMPS, MODES, elements), BF),
            side, side, side, side,
        ],
        scratch_shapes=[
            pltpu.VMEM((CORNERS * COMPS, CORNERS * DOFS, BLOCK), F32),
            pltpu.VMEM((CORNERS, ROWS, BLOCK), F32),
            pltpu.VMEM((TALL, LANES), F32),
        ],
        compiler_params=params(),
        cost_estimate=pl.CostEstimate(flops=10**10, bytes_accessed=10**7, transcendentals=0),
        name="stress",
    )(modes_disp, recovery, connect)
    got_w = ring(part_e, "px", 1)
    got_e = ring(part_w, "px", -1)
    got_s = ring(part_n, "py", 1)
    got_n = ring(part_s, "py", -1)
    big = 2 * BLOCK
    near, ids = pl.pallas_call(
        scatter_kernel,
        grid=(elements // big,),
        in_specs=[
            pl.BlockSpec((CORNERS * COMPS, MODES, big), lambda i: (0, 0, i)),
            pl.BlockSpec((CORNERS, big), lambda i: (0, i)),
            whole(CORNERS, elements),
            whole(1, reads),
            whole(CORNERS * COMPS, reads),
        ],
        out_specs=[whole(CORNERS, MODES + 8, reads), whole(CORNERS, reads)],
        out_shape=[
            jax.ShapeDtypeStruct((CORNERS, MODES + 8, reads), F32),
            jax.ShapeDtypeStruct((CORNERS, reads), jnp.int32),
        ],
        scratch_shapes=[
            pltpu.VMEM((tiles, TILE, LANES), jnp.int16),
            pltpu.VMEM((tiles, TALL, TILE), F32),
        ],
        compiler_params=params(),
        cost_estimate=pl.CostEstimate(flops=10**10, bytes_accessed=10**7, transcendentals=0),
        name="scatter",
    )(stress, connect, connect, read_elem.reshape(1, reads), read_wts)
    outgoing = pl.pallas_call(
        functools.partial(readout_kernel, zones=zones, cap=cap),
        in_specs=[full] * 8,
        out_specs=full,
        out_shape=jax.ShapeDtypeStruct((zones * cap, LANES), BF),
        compiler_params=params(),
        name="readout",
    )(near, ids, got_w, got_e, got_s, got_n, read_wts, zone.reshape(1, reads))
    arrived = lax.all_to_all(
        outgoing.reshape(zones, cap, LANES), ("px", "py"), split_axis=0, concat_axis=0, tiled=True
    ).reshape(zones * cap, LANES)
    deep = jnp.pad(response, ((0, LANES - MODES), (0, 0)))
    return jnp.dot(arrived, deep, preferred_element_type=F32).astype(BF)


def solution(mesh):
    placed = (
        P(None, ("px", "py")),
        P(None, None, ("px", "py")),
        P(None, ("px", "py")),
        P(("px", "py")),
        P(None, ("px", "py")),
        P(("px", "py"), None),
        P(),
    )
    return jax.shard_map(
        per_device, mesh=mesh, in_specs=placed, out_specs=P(("px", "py"), None), check_vma=False
    )
```

```python
import functools

import jax
import jax.numpy as jnp
from jax import lax
from jax.experimental import pallas as pl
from jax.experimental.pallas import tpu as pltpu
from jax.sharding import PartitionSpec as P

MODES = 48
CORNERS = 4
DOFS = 6
COMPS = 6
BORDER = 32
ROWS = COMPS * MODES
TALL = ROWS + 16
WIDE = 384
BLOCK = 256
TILE = 256
GROUP = 12
STRIP = 16
UNROLL = 4
LANES = 128
BF = jnp.bfloat16
F32 = jnp.float32


def hot(mask):
    return jnp.where(mask, jnp.ones((), BF), jnp.zeros((), BF))


def rows16(row):
    return jnp.broadcast_to(row, (16, row.shape[1])).astype(jnp.int16)


def tall16(row, count):
    width = row.shape[1]
    return jnp.broadcast_to(row[None], (count // 16, 16, width)).reshape(count, width)


def line16(connect):
    return jnp.concatenate([rows16(connect[c : c + 1, :]) for c in range(CORNERS)], axis=1)


def dot_rows(x, y):
    return lax.dot_general(x, y, (((1,), (1,)), ((), ())), preferred_element_type=F32)


def with_ones(stress):
    count = stress.shape[2]
    sides = [stress[c * COMPS : (c + 1) * COMPS].reshape(ROWS, count) for c in range(CORNERS)]
    return jnp.concatenate(
        [jnp.concatenate(sides, axis=1), jnp.ones((TALL - ROWS, CORNERS * count), BF)], axis=0
    )


def stress_kernel(modes, recovery, connect, stress, side_w, side_e, side_s, side_n, rf, vc, accb):
    step = pl.program_id(0)
    nodes = modes.shape[1]

    @pl.when(step == 0)
    def _():
        accb[...] = jnp.zeros_like(accb)

    rf[...] = recovery[...].astype(F32)
    for corner in range(CORNERS):
        row = tall16(rows16(connect[corner : corner + 1, :]), nodes)
        ids = lax.broadcasted_iota(jnp.int16, (nodes, BLOCK), 0)
        vc[corner] = jnp.dot(modes[...], hot(ids == row), preferred_element_type=F32)

    for half in range(BLOCK // LANES):
        lanes = slice(half * LANES, (half + 1) * LANES)

        @pl.loop(0, CORNERS * COMPS // GROUP)
        def _(t):
            first = t * GROUP
            for part in range(MODES // STRIP):
                done = []
                for thin in range(0, STRIP, 8):
                    sums = [None] * GROUP
                    for j in range(CORNERS * DOFS):
                        base = (j % DOFS) * MODES + part * STRIP + thin
                        moved = vc[j // DOFS, base : base + 8, lanes]
                        for q in range(GROUP):
                            term = rf[first + q, j : j + 1, lanes] * moved
                            sums[q] = term if j == 0 else sums[q] + term
                    done.append(sums)
                for q in range(GROUP):
                    both = jnp.concatenate([sums[q] for sums in done], axis=0)
                    stress[first + q, part * STRIP : (part + 1) * STRIP, lanes] = both.astype(BF)

    ids = lax.broadcasted_iota(jnp.int16, (LANES, CORNERS * BLOCK), 0)
    accb[...] += dot_rows(with_ones(stress[...]), hot(ids == tall16(line16(connect), LANES)))

    @pl.when(step == pl.num_programs(0) - 1)
    def _():
        tall = jnp.concatenate([accb[...], jnp.zeros((WIDE - TALL, LANES), F32)], axis=0)
        turned = jnp.transpose(tall)
        count = turned[:, ROWS : ROWS + 1].astype(jnp.int32)
        high = lax.shift_right_logical(count, 7)
        low = (count - high * 128).astype(F32)
        high = high.astype(F32)
        lane = lax.broadcasted_iota(jnp.int32, (LANES, WIDE), 1)
        out = jnp.where(lane < ROWS, turned, 0.0)
        out = jnp.where(lane == ROWS, high, out)
        out = jnp.where(lane == ROWS + 1, low, out).astype(BF)
        for side, ref in enumerate((side_w, side_e, side_s, side_n)):
            ref[...] = out[side * BORDER : (side + 1) * BORDER, :]


def weighted(values, shares, c, at):
    total = None
    for k in range(COMPS):
        term = shares[c * COMPS + k : c * COMPS + k + 1, at] * values[k * MODES : (k + 1) * MODES]
        total = term if k == 0 else total + term
    return total


def scatter_kernel(stress, connect, whole, elems, weights, spots, ids_out, qcol, acc):
    step = pl.program_id(0)
    tiles = acc.shape[0]
    nodes = whole.shape[1]
    reads = elems.shape[1]
    halves = reads // TILE

    @pl.when(step == 0)
    def _():
        ids = whole[...]
        high = lax.shift_right_logical(ids, 4)
        low = ids - high * 16
        split = jnp.concatenate([high, low], axis=0).astype(F32)
        split = jnp.concatenate([split, jnp.zeros_like(split)], axis=0).astype(BF)
        iota = lax.broadcasted_iota(jnp.int16, (nodes, reads), 0)
        mask = iota == tall16(rows16(elems[...]), nodes)
        got = jnp.dot(split, hot(mask), preferred_element_type=F32)
        found = (got[0:4] * 16.0 + got[4:8]).astype(jnp.int32)
        ids_out[...] = found
        turned = jnp.transpose(jnp.concatenate([found, found], axis=0))
        for tile in range(tiles):
            c, part = tile // halves, tile % halves
            column = turned[part * TILE : (part + 1) * TILE, c : c + 1]
            qcol[tile] = jnp.broadcast_to(column, (TILE, LANES)).astype(jnp.int16)
        acc[...] = jnp.zeros_like(acc)

    @pl.loop(0, tiles // UNROLL)
    def _(t):
        lhs = with_ones(stress[...])
        line = tall16(line16(connect), TILE)
        for u in range(UNROLL):
            ids = qcol[t * UNROLL + u]
            mask = jnp.concatenate([ids] * (line.shape[1] // LANES), axis=1) == line
            acc[t * UNROLL + u] += dot_rows(lhs, hot(mask))

    @pl.when(step == pl.num_programs(0) - 1)
    def _():
        for tile in range(tiles):
            c, part = tile // halves, tile % halves
            at = slice(part * TILE, (part + 1) * TILE)
            spots[c, 0:MODES, at] = weighted(acc[tile, 0:ROWS, :], weights, c, at)
            spots[c, MODES : MODES + 8, at] = acc[tile, ROWS : ROWS + 8, :]


def readout_kernel(near, ids, got_w, got_e, got_s, got_n, weights, zone, out, *, zones, cap):
    reads = ids.shape[1]
    halves = reads // TILE
    i, j = lax.axis_index("px"), lax.axis_index("py")
    flags = (i > 0, i < lax.axis_size("px") - 1, j > 0, j < lax.axis_size("py") - 1)
    pieces = []
    for side, ref in enumerate((got_w, got_e, got_s, got_n)):
        value = ref[...].astype(F32)
        pieces.append(jnp.where(flags[side], value, jnp.zeros_like(value)))
    border = jnp.transpose(jnp.concatenate(pieces, axis=0))[0:TALL].astype(BF)
    spots = [None] * halves
    iota = lax.broadcasted_iota(jnp.int32, (4 * BORDER, TILE), 0)
    for part in range(halves):
        at = slice(part * TILE, (part + 1) * TILE)
        for c in range(CORNERS):
            mask = iota == ids[c : c + 1, at]
            more = jnp.dot(border, mask.astype(F32).astype(BF), preferred_element_type=F32)
            count = near[c, MODES : MODES + 1, at] + (
                more[ROWS : ROWS + 1] * 128.0 + more[ROWS + 1 : ROWS + 2]
            )
            term = (near[c, 0:MODES, at] + weighted(more, weights, c, at)) / count
            spots[part] = term if c == 0 else spots[part] + term
    spot = jnp.concatenate(spots, axis=1)
    spot = jnp.concatenate([spot, jnp.zeros((LANES - MODES, reads), F32)], axis=0)
    spot = jnp.transpose(spot).astype(BF)
    row = zone[...]
    column = jnp.transpose(jnp.broadcast_to(row, (8, reads)))[:, 0:1]
    at_row = lax.broadcasted_iota(jnp.int32, (reads, reads), 1)
    at_col = lax.broadcasted_iota(jnp.int32, (reads, reads), 0)
    same = jnp.where((column == row) & (at_col < at_row), 1.0, 0.0)
    rank = jnp.sum(same, axis=0, keepdims=True).astype(jnp.int32)
    slot = row * cap + rank
    chunk = 256
    for base in range(0, zones * cap, chunk):
        chosen = lax.broadcasted_iota(jnp.int32, (chunk, reads), 0) + base == slot
        out[base : base + chunk, :] = jnp.dot(
            chosen.astype(F32).astype(BF), spot, preferred_element_type=F32
        ).astype(BF)


def ring(x, axis, by):
    count = lax.axis_size(axis)
    return lax.ppermute(x, axis, [(i, (i + by) % count) for i in range(count)])


def params():
    return pltpu.CompilerParams(vmem_limit_bytes=56 * 2**20)


def per_device(modes_disp, recovery, connect, read_elem, read_wts, zone, response):
    elements = connect.shape[1]
    nodes = modes_disp.shape[1]
    reads = read_elem.shape[0]
    px, py = lax.axis_size("px"), lax.axis_size("py")
    zones = px * py
    cap = max(2, 2 * reads // zones)
    tiles = CORNERS * reads // TILE
    full = pl.BlockSpec(memory_space=pltpu.VMEM)
    side = jax.ShapeDtypeStruct((BORDER, WIDE), BF)
    whole = lambda *shape: pl.BlockSpec(shape, lambda i: (0,) * len(shape))
    stress, part_w, part_e, part_s, part_n = pl.pallas_call(
        stress_kernel,
        grid=(elements // BLOCK,),
        in_specs=[
            whole(ROWS, nodes),
            pl.BlockSpec((CORNERS * COMPS, CORNERS * DOFS, BLOCK), lambda i: (0, 0, i)),
            pl.BlockSpec((CORNERS, BLOCK), lambda i: (0, i)),
        ],
        out_specs=[pl.BlockSpec((CORNERS * COMPS, MODES, BLOCK), lambda i: (0, 0, i))]
        + [whole(BORDER, WIDE)] * 4,
        out_shape=[
            jax.ShapeDtypeStruct((CORNERS * COMPS, MODES, elements), BF),
            side, side, side, side,
        ],
        scratch_shapes=[
            pltpu.VMEM((CORNERS * COMPS, CORNERS * DOFS, BLOCK), F32),
            pltpu.VMEM((CORNERS, ROWS, BLOCK), F32),
            pltpu.VMEM((TALL, LANES), F32),
        ],
        compiler_params=params(),
        cost_estimate=pl.CostEstimate(flops=10**10, bytes_accessed=10**7, transcendentals=0),
        name="stress",
    )(modes_disp, recovery, connect)
    got_w = ring(part_e, "px", 1)
    got_e = ring(part_w, "px", -1)
    got_s = ring(part_n, "py", 1)
    got_n = ring(part_s, "py", -1)
    big = 2 * BLOCK
    near, ids = pl.pallas_call(
        scatter_kernel,
        grid=(elements // big,),
        in_specs=[
            pl.BlockSpec((CORNERS * COMPS, MODES, big), lambda i: (0, 0, i)),
            pl.BlockSpec((CORNERS, big), lambda i: (0, i)),
            whole(CORNERS, elements),
            whole(1, reads),
            whole(CORNERS * COMPS, reads),
        ],
        out_specs=[whole(CORNERS, MODES + 8, reads), whole(CORNERS, reads)],
        out_shape=[
            jax.ShapeDtypeStruct((CORNERS, MODES + 8, reads), F32),
            jax.ShapeDtypeStruct((CORNERS, reads), jnp.int32),
        ],
        scratch_shapes=[
            pltpu.VMEM((tiles, TILE, LANES), jnp.int16),
            pltpu.VMEM((tiles, TALL, TILE), F32),
        ],
        compiler_params=params(),
        cost_estimate=pl.CostEstimate(flops=10**10, bytes_accessed=10**7, transcendentals=0),
        name="scatter",
    )(stress, connect, connect, read_elem.reshape(1, reads), read_wts)
    outgoing = pl.pallas_call(
        functools.partial(readout_kernel, zones=zones, cap=cap),
        in_specs=[full] * 8,
        out_specs=full,
        out_shape=jax.ShapeDtypeStruct((zones * cap, LANES), BF),
        compiler_params=params(),
        name="readout",
    )(near, ids, got_w, got_e, got_s, got_n, read_wts, zone.reshape(1, reads))
    arrived = lax.all_to_all(
        outgoing.reshape(zones, cap, LANES), ("px", "py"), split_axis=0, concat_axis=0, tiled=True
    ).reshape(zones * cap, LANES)
    deep = jnp.pad(response, ((0, LANES - MODES), (0, 0)))
    return jnp.dot(arrived, deep, preferred_element_type=F32).astype(BF)


def solution(mesh):
    placed = (
        P(None, ("px", "py")),
        P(None, None, ("px", "py")),
        P(None, ("px", "py")),
        P(("px", "py")),
        P(None, ("px", "py")),
        P(("px", "py"), None),
        P(),
    )
    return jax.shard_map(
        per_device, mesh=mesh, in_specs=placed, out_specs=P(("px", "py"), None), check_vma=False
    )
```

```python
import functools

import jax
import jax.numpy as jnp
from jax import lax
from jax.experimental import pallas as pl
from jax.experimental.pallas import tpu as pltpu
from jax.sharding import PartitionSpec as P

MODES = 48
CORNERS = 4
DOFS = 6
COMPS = 6
BORDER = 32
ROWS = COMPS * MODES
TALL = ROWS + 16
WIDE = 384
BLOCK = 256
TILE = 256
GROUP = 12
STRIP = 16
UNROLL = 8
LANES = 128
BF = jnp.bfloat16
F32 = jnp.float32


def hot(mask):
    return jnp.where(mask, jnp.ones((), BF), jnp.zeros((), BF))


def rows16(row):
    return jnp.broadcast_to(row, (16, row.shape[1])).astype(jnp.int16)


def tall16(row, count):
    width = row.shape[1]
    return jnp.broadcast_to(row[None], (count // 16, 16, width)).reshape(count, width)


def line16(connect):
    return jnp.concatenate([rows16(connect[c : c + 1, :]) for c in range(CORNERS)], axis=1)


def dot_rows(x, y):
    return lax.dot_general(x, y, (((1,), (1,)), ((), ())), preferred_element_type=F32)


def with_ones(stress):
    count = stress.shape[2]
    sides = [stress[c * COMPS : (c + 1) * COMPS].reshape(ROWS, count) for c in range(CORNERS)]
    return jnp.concatenate(
        [jnp.concatenate(sides, axis=1), jnp.ones((TALL - ROWS, CORNERS * count), BF)], axis=0
    )


def stress_kernel(modes, recovery, connect, stress, side_w, side_e, side_s, side_n, rf, vc, accb):
    step = pl.program_id(0)
    nodes = modes.shape[1]

    @pl.when(step == 0)
    def _():
        accb[...] = jnp.zeros_like(accb)

    halves = BLOCK // LANES
    for half in range(halves):
        rf[half] = recovery[:, :, half * LANES : (half + 1) * LANES].astype(F32)
    for corner in range(CORNERS):
        row = tall16(rows16(connect[corner : corner + 1, :]), nodes)
        ids = lax.broadcasted_iota(jnp.int16, (nodes, BLOCK), 0)
        moved = jnp.dot(modes[...], hot(ids == row), preferred_element_type=F32)
        for half in range(halves):
            vc[half, corner] = moved[:, half * LANES : (half + 1) * LANES]

    for half in range(halves):
        lanes = slice(half * LANES, (half + 1) * LANES)

        @pl.loop(0, CORNERS * COMPS // GROUP)
        def _(t):
            first = t * GROUP
            for part in range(MODES // STRIP):
                done = []
                for thin in range(0, STRIP, 8):
                    sums = [None] * GROUP
                    for j in range(CORNERS * DOFS):
                        base = (j % DOFS) * MODES + part * STRIP + thin
                        moved = vc[half, j // DOFS, base : base + 8, :]
                        for q in range(GROUP):
                            term = rf[half, first + q, j : j + 1, :] * moved
                            sums[q] = term if j == 0 else sums[q] + term
                    done.append(sums)
                for q in range(GROUP):
                    both = jnp.concatenate([sums[q] for sums in done], axis=0)
                    stress[first + q, part * STRIP : (part + 1) * STRIP, lanes] = both.astype(BF)

    ids = lax.broadcasted_iota(jnp.int16, (LANES, CORNERS * BLOCK), 0)
    accb[...] += dot_rows(with_ones(stress[...]), hot(ids == tall16(line16(connect), LANES)))

    @pl.when(step == pl.num_programs(0) - 1)
    def _():
        tall = jnp.concatenate([accb[...], jnp.zeros((WIDE - TALL, LANES), F32)], axis=0)
        turned = jnp.transpose(tall)
        count = turned[:, ROWS : ROWS + 1].astype(jnp.int32)
        high = lax.shift_right_logical(count, 7)
        low = (count - high * 128).astype(F32)
        high = high.astype(F32)
        lane = lax.broadcasted_iota(jnp.int32, (LANES, WIDE), 1)
        out = jnp.where(lane < ROWS, turned, 0.0)
        out = jnp.where(lane == ROWS, high, out)
        out = jnp.where(lane == ROWS + 1, low, out).astype(BF)
        for side, ref in enumerate((side_w, side_e, side_s, side_n)):
            ref[...] = out[side * BORDER : (side + 1) * BORDER, :]


def weighted(values, shares, c, at):
    total = None
    for k in range(COMPS):
        term = shares[c * COMPS + k : c * COMPS + k + 1, at] * values[k * MODES : (k + 1) * MODES]
        total = term if k == 0 else total + term
    return total


def scatter_kernel(stress, connect, whole, elems, weights, spots, ids_out, qcol, acc):
    step = pl.program_id(0)
    tiles = acc.shape[0]
    nodes = whole.shape[1]
    reads = elems.shape[1]
    halves = reads // TILE

    @pl.when(step == 0)
    def _():
        ids = whole[...]
        high = lax.shift_right_logical(ids, 4)
        low = ids - high * 16
        split = jnp.concatenate([high, low], axis=0).astype(F32)
        split = jnp.concatenate([split, jnp.zeros_like(split)], axis=0).astype(BF)
        iota = lax.broadcasted_iota(jnp.int16, (nodes, reads), 0)
        mask = iota == tall16(rows16(elems[...]), nodes)
        got = jnp.dot(split, hot(mask), preferred_element_type=F32)
        found = (got[0:4] * 16.0 + got[4:8]).astype(jnp.int32)
        ids_out[...] = found
        turned = jnp.transpose(jnp.concatenate([found, found], axis=0))
        for tile in range(tiles):
            c, part = tile // halves, tile % halves
            column = turned[part * TILE : (part + 1) * TILE, c : c + 1]
            qcol[tile] = jnp.broadcast_to(column, (TILE, LANES)).astype(jnp.int16)
        acc[...] = jnp.zeros_like(acc)

    @pl.loop(0, tiles // UNROLL)
    def _(t):
        lhs = with_ones(stress[...])
        line = tall16(line16(connect), TILE)
        for u in range(UNROLL):
            ids = qcol[t * UNROLL + u]
            mask = jnp.concatenate([ids] * (line.shape[1] // LANES), axis=1) == line
            acc[t * UNROLL + u] += dot_rows(lhs, hot(mask))

    @pl.when(step == pl.num_programs(0) - 1)
    def _():
        for tile in range(tiles):
            c, part = tile // halves, tile % halves
            at = slice(part * TILE, (part + 1) * TILE)
            spots[c, 0:MODES, at] = weighted(acc[tile, 0:ROWS, :], weights, c, at)
            spots[c, MODES : MODES + 8, at] = acc[tile, ROWS : ROWS + 8, :]


def readout_kernel(near, ids, got_w, got_e, got_s, got_n, weights, zone, out, *, zones, cap):
    reads = ids.shape[1]
    halves = reads // TILE
    i, j = lax.axis_index("px"), lax.axis_index("py")
    flags = (i > 0, i < lax.axis_size("px") - 1, j > 0, j < lax.axis_size("py") - 1)
    pieces = []
    for side, ref in enumerate((got_w, got_e, got_s, got_n)):
        value = ref[...].astype(F32)
        pieces.append(jnp.where(flags[side], value, jnp.zeros_like(value)))
    border = jnp.transpose(jnp.concatenate(pieces, axis=0))[0:TALL].astype(BF)
    spots = [None] * halves
    iota = lax.broadcasted_iota(jnp.int32, (4 * BORDER, TILE), 0)
    for part in range(halves):
        at = slice(part * TILE, (part + 1) * TILE)
        for c in range(CORNERS):
            mask = iota == ids[c : c + 1, at]
            more = jnp.dot(border, mask.astype(F32).astype(BF), preferred_element_type=F32)
            count = near[c, MODES : MODES + 1, at] + (
                more[ROWS : ROWS + 1] * 128.0 + more[ROWS + 1 : ROWS + 2]
            )
            term = (near[c, 0:MODES, at] + weighted(more, weights, c, at)) / count
            spots[part] = term if c == 0 else spots[part] + term
    spot = jnp.concatenate(spots, axis=1)
    spot = jnp.concatenate([spot, jnp.zeros((LANES - MODES, reads), F32)], axis=0)
    spot = jnp.transpose(spot).astype(BF)
    row = zone[...]
    column = jnp.transpose(jnp.broadcast_to(row, (8, reads)))[:, 0:1]
    at_row = lax.broadcasted_iota(jnp.int32, (reads, reads), 1)
    at_col = lax.broadcasted_iota(jnp.int32, (reads, reads), 0)
    same = jnp.where((column == row) & (at_col < at_row), 1.0, 0.0)
    rank = jnp.sum(same, axis=0, keepdims=True).astype(jnp.int32)
    slot = row * cap + rank
    chunk = 256
    for base in range(0, zones * cap, chunk):
        chosen = lax.broadcasted_iota(jnp.int32, (chunk, reads), 0) + base == slot
        out[base : base + chunk, :] = jnp.dot(
            chosen.astype(F32).astype(BF), spot, preferred_element_type=F32
        ).astype(BF)


def ring(x, axis, by):
    count = lax.axis_size(axis)
    return lax.ppermute(x, axis, [(i, (i + by) % count) for i in range(count)])


def params():
    return pltpu.CompilerParams(vmem_limit_bytes=56 * 2**20)


def per_device(modes_disp, recovery, connect, read_elem, read_wts, zone, response):
    elements = connect.shape[1]
    nodes = modes_disp.shape[1]
    reads = read_elem.shape[0]
    px, py = lax.axis_size("px"), lax.axis_size("py")
    zones = px * py
    cap = max(2, 2 * reads // zones)
    tiles = CORNERS * reads // TILE
    full = pl.BlockSpec(memory_space=pltpu.VMEM)
    side = jax.ShapeDtypeStruct((BORDER, WIDE), BF)
    whole = lambda *shape: pl.BlockSpec(shape, lambda i: (0,) * len(shape))
    stress, part_w, part_e, part_s, part_n = pl.pallas_call(
        stress_kernel,
        grid=(elements // BLOCK,),
        in_specs=[
            whole(ROWS, nodes),
            pl.BlockSpec((CORNERS * COMPS, CORNERS * DOFS, BLOCK), lambda i: (0, 0, i)),
            pl.BlockSpec((CORNERS, BLOCK), lambda i: (0, i)),
        ],
        out_specs=[pl.BlockSpec((CORNERS * COMPS, MODES, BLOCK), lambda i: (0, 0, i))]
        + [whole(BORDER, WIDE)] * 4,
        out_shape=[
            jax.ShapeDtypeStruct((CORNERS * COMPS, MODES, elements), BF),
            side, side, side, side,
        ],
        scratch_shapes=[
            pltpu.VMEM((BLOCK // LANES, CORNERS * COMPS, CORNERS * DOFS, LANES), F32),
            pltpu.VMEM((BLOCK // LANES, CORNERS, ROWS, LANES), F32),
            pltpu.VMEM((TALL, LANES), F32),
        ],
        compiler_params=params(),
        cost_estimate=pl.CostEstimate(flops=10**10, bytes_accessed=10**7, transcendentals=0),
        name="stress",
    )(modes_disp, recovery, connect)
    got_w = ring(part_e, "px", 1)
    got_e = ring(part_w, "px", -1)
    got_s = ring(part_n, "py", 1)
    got_n = ring(part_s, "py", -1)
    big = 2 * BLOCK
    near, ids = pl.pallas_call(
        scatter_kernel,
        grid=(elements // big,),
        in_specs=[
            pl.BlockSpec((CORNERS * COMPS, MODES, big), lambda i: (0, 0, i)),
            pl.BlockSpec((CORNERS, big), lambda i: (0, i)),
            whole(CORNERS, elements),
            whole(1, reads),
            whole(CORNERS * COMPS, reads),
        ],
        out_specs=[whole(CORNERS, MODES + 8, reads), whole(CORNERS, reads)],
        out_shape=[
            jax.ShapeDtypeStruct((CORNERS, MODES + 8, reads), F32),
            jax.ShapeDtypeStruct((CORNERS, reads), jnp.int32),
        ],
        scratch_shapes=[
            pltpu.VMEM((tiles, TILE, LANES), jnp.int16),
            pltpu.VMEM((tiles, TALL, TILE), F32),
        ],
        compiler_params=params(),
        cost_estimate=pl.CostEstimate(flops=10**10, bytes_accessed=10**7, transcendentals=0),
        name="scatter",
    )(stress, connect, connect, read_elem.reshape(1, reads), read_wts)
    outgoing = pl.pallas_call(
        functools.partial(readout_kernel, zones=zones, cap=cap),
        in_specs=[full] * 8,
        out_specs=full,
        out_shape=jax.ShapeDtypeStruct((zones * cap, LANES), BF),
        compiler_params=params(),
        name="readout",
    )(near, ids, got_w, got_e, got_s, got_n, read_wts, zone.reshape(1, reads))
    arrived = lax.all_to_all(
        outgoing.reshape(zones, cap, LANES), ("px", "py"), split_axis=0, concat_axis=0, tiled=True
    ).reshape(zones * cap, LANES)
    deep = jnp.pad(response, ((0, LANES - MODES), (0, 0)))
    return jnp.dot(arrived, deep, preferred_element_type=F32).astype(BF)


def solution(mesh):
    placed = (
        P(None, ("px", "py")),
        P(None, None, ("px", "py")),
        P(None, ("px", "py")),
        P(("px", "py")),
        P(None, ("px", "py")),
        P(("px", "py"), None),
        P(),
    )
    return jax.shard_map(
        per_device, mesh=mesh, in_specs=placed, out_specs=P(("px", "py"), None), check_vma=False
    )
```

```python
import functools

import jax
import jax.numpy as jnp
from jax import lax
from jax.experimental import pallas as pl
from jax.experimental.pallas import tpu as pltpu
from jax.sharding import PartitionSpec as P

MODES = 48
CORNERS = 4
DOFS = 6
COMPS = 6
BORDER = 32
ROWS = COMPS * MODES
TALL = ROWS + 16
WIDE = 384
BLOCK = 512
TILE = 256
GROUP = 12
STRIP = 16
UNROLL = 8
LANES = 128
BF = jnp.bfloat16
F32 = jnp.float32


def hot(mask):
    return jnp.where(mask, jnp.ones((), BF), jnp.zeros((), BF))


def rows16(row):
    return jnp.broadcast_to(row, (16, row.shape[1])).astype(jnp.int16)


def tall16(row, count):
    width = row.shape[1]
    return jnp.broadcast_to(row[None], (count // 16, 16, width)).reshape(count, width)


def line16(connect):
    return jnp.concatenate([rows16(connect[c : c + 1, :]) for c in range(CORNERS)], axis=1)


def dot_rows(x, y):
    return lax.dot_general(x, y, (((1,), (1,)), ((), ())), preferred_element_type=F32)


def with_ones(stress):
    count = stress.shape[2]
    sides = [stress[c * COMPS : (c + 1) * COMPS].reshape(ROWS, count) for c in range(CORNERS)]
    return jnp.concatenate(
        [jnp.concatenate(sides, axis=1), jnp.ones((TALL - ROWS, CORNERS * count), BF)], axis=0
    )


def stress_kernel(modes, recovery, connect, stress, side_w, side_e, side_s, side_n, rf, vc, accb):
    step = pl.program_id(0)
    nodes = modes.shape[1]

    @pl.when(step == 0)
    def _():
        accb[...] = jnp.zeros_like(accb)

    halves = BLOCK // LANES
    for half in range(halves):
        rf[half] = recovery[:, :, half * LANES : (half + 1) * LANES].astype(F32)
    for corner in range(CORNERS):
        row = tall16(rows16(connect[corner : corner + 1, :]), nodes)
        ids = lax.broadcasted_iota(jnp.int16, (nodes, BLOCK), 0)
        moved = jnp.dot(modes[...], hot(ids == row), preferred_element_type=F32)
        for half in range(halves):
            vc[half, corner] = moved[:, half * LANES : (half + 1) * LANES]

    for half in range(halves):
        lanes = slice(half * LANES, (half + 1) * LANES)

        @pl.loop(0, CORNERS * COMPS // GROUP)
        def _(t):
            first = t * GROUP
            for part in range(MODES // STRIP):
                done = []
                for thin in range(0, STRIP, 8):
                    sums = [None] * GROUP
                    for j in range(CORNERS * DOFS):
                        base = (j % DOFS) * MODES + part * STRIP + thin
                        moved = vc[half, j // DOFS, base : base + 8, :]
                        for q in range(GROUP):
                            term = rf[half, first + q, j : j + 1, :] * moved
                            sums[q] = term if j == 0 else sums[q] + term
                    done.append(sums)
                for q in range(GROUP):
                    both = jnp.concatenate([sums[q] for sums in done], axis=0)
                    stress[first + q, part * STRIP : (part + 1) * STRIP, lanes] = both.astype(BF)

    ids = lax.broadcasted_iota(jnp.int16, (LANES, CORNERS * BLOCK), 0)
    accb[...] += dot_rows(with_ones(stress[...]), hot(ids == tall16(line16(connect), LANES)))

    @pl.when(step == pl.num_programs(0) - 1)
    def _():
        tall = jnp.concatenate([accb[...], jnp.zeros((WIDE - TALL, LANES), F32)], axis=0)
        turned = jnp.transpose(tall)
        count = turned[:, ROWS : ROWS + 1].astype(jnp.int32)
        high = lax.shift_right_logical(count, 7)
        low = (count - high * 128).astype(F32)
        high = high.astype(F32)
        lane = lax.broadcasted_iota(jnp.int32, (LANES, WIDE), 1)
        out = jnp.where(lane < ROWS, turned, 0.0)
        out = jnp.where(lane == ROWS, high, out)
        out = jnp.where(lane == ROWS + 1, low, out).astype(BF)
        for side, ref in enumerate((side_w, side_e, side_s, side_n)):
            ref[...] = out[side * BORDER : (side + 1) * BORDER, :]


def weighted(values, shares, c, at):
    total = None
    for k in range(COMPS):
        term = shares[c * COMPS + k : c * COMPS + k + 1, at] * values[k * MODES : (k + 1) * MODES]
        total = term if k == 0 else total + term
    return total


def scatter_kernel(stress, connect, whole, elems, weights, spots, ids_out, qcol, acc):
    step = pl.program_id(0)
    tiles = acc.shape[0]
    nodes = whole.shape[1]
    reads = elems.shape[1]
    halves = reads // TILE

    @pl.when(step == 0)
    def _():
        ids = whole[...]
        high = lax.shift_right_logical(ids, 4)
        low = ids - high * 16
        split = jnp.concatenate([high, low], axis=0).astype(F32)
        split = jnp.concatenate([split, jnp.zeros_like(split)], axis=0).astype(BF)
        iota = lax.broadcasted_iota(jnp.int16, (nodes, reads), 0)
        mask = iota == tall16(rows16(elems[...]), nodes)
        got = jnp.dot(split, hot(mask), preferred_element_type=F32)
        found = (got[0:4] * 16.0 + got[4:8]).astype(jnp.int32)
        ids_out[...] = found
        turned = jnp.transpose(jnp.concatenate([found, found], axis=0))
        for tile in range(tiles):
            c, part = tile // halves, tile % halves
            column = turned[part * TILE : (part + 1) * TILE, c : c + 1]
            qcol[tile] = jnp.broadcast_to(column, (TILE, LANES)).astype(jnp.int16)
        acc[...] = jnp.zeros_like(acc)

    @pl.loop(0, tiles // UNROLL)
    def _(t):
        lhs = with_ones(stress[...])
        line = tall16(line16(connect), TILE)
        for u in range(UNROLL):
            ids = qcol[t * UNROLL + u]
            mask = jnp.concatenate([ids] * (line.shape[1] // LANES), axis=1) == line
            acc[t * UNROLL + u] += dot_rows(lhs, hot(mask))

    @pl.when(step == pl.num_programs(0) - 1)
    def _():
        for tile in range(tiles):
            c, part = tile // halves, tile % halves
            at = slice(part * TILE, (part + 1) * TILE)
            spots[c, 0:MODES, at] = weighted(acc[tile, 0:ROWS, :], weights, c, at)
            spots[c, MODES : MODES + 8, at] = acc[tile, ROWS : ROWS + 8, :]


def readout_kernel(near, ids, got_w, got_e, got_s, got_n, weights, zone, out, *, zones, cap):
    reads = ids.shape[1]
    halves = reads // TILE
    i, j = lax.axis_index("px"), lax.axis_index("py")
    flags = (i > 0, i < lax.axis_size("px") - 1, j > 0, j < lax.axis_size("py") - 1)
    pieces = []
    for side, ref in enumerate((got_w, got_e, got_s, got_n)):
        value = ref[...].astype(F32)
        pieces.append(jnp.where(flags[side], value, jnp.zeros_like(value)))
    border = jnp.transpose(jnp.concatenate(pieces, axis=0))[0:TALL].astype(BF)
    spots = [None] * halves
    iota = lax.broadcasted_iota(jnp.int32, (4 * BORDER, TILE), 0)
    for part in range(halves):
        at = slice(part * TILE, (part + 1) * TILE)
        for c in range(CORNERS):
            mask = iota == ids[c : c + 1, at]
            more = jnp.dot(border, mask.astype(F32).astype(BF), preferred_element_type=F32)
            count = near[c, MODES : MODES + 1, at] + (
                more[ROWS : ROWS + 1] * 128.0 + more[ROWS + 1 : ROWS + 2]
            )
            term = (near[c, 0:MODES, at] + weighted(more, weights, c, at)) / count
            spots[part] = term if c == 0 else spots[part] + term
    spot = jnp.concatenate(spots, axis=1)
    spot = jnp.concatenate([spot, jnp.zeros((LANES - MODES, reads), F32)], axis=0)
    spot = jnp.transpose(spot).astype(BF)
    row = zone[...]
    column = jnp.transpose(jnp.broadcast_to(row, (8, reads)))[:, 0:1]
    at_row = lax.broadcasted_iota(jnp.int32, (reads, reads), 1)
    at_col = lax.broadcasted_iota(jnp.int32, (reads, reads), 0)
    same = jnp.where((column == row) & (at_col < at_row), 1.0, 0.0)
    rank = jnp.sum(same, axis=0, keepdims=True).astype(jnp.int32)
    slot = row * cap + rank
    chunk = 256
    for base in range(0, zones * cap, chunk):
        chosen = lax.broadcasted_iota(jnp.int32, (chunk, reads), 0) + base == slot
        out[base : base + chunk, :] = jnp.dot(
            chosen.astype(F32).astype(BF), spot, preferred_element_type=F32
        ).astype(BF)


def ring(x, axis, by):
    count = lax.axis_size(axis)
    return lax.ppermute(x, axis, [(i, (i + by) % count) for i in range(count)])


def params():
    return pltpu.CompilerParams(vmem_limit_bytes=56 * 2**20)


def per_device(modes_disp, recovery, connect, read_elem, read_wts, zone, response):
    elements = connect.shape[1]
    nodes = modes_disp.shape[1]
    reads = read_elem.shape[0]
    px, py = lax.axis_size("px"), lax.axis_size("py")
    zones = px * py
    cap = max(2, 2 * reads // zones)
    tiles = CORNERS * reads // TILE
    full = pl.BlockSpec(memory_space=pltpu.VMEM)
    side = jax.ShapeDtypeStruct((BORDER, WIDE), BF)
    whole = lambda *shape: pl.BlockSpec(shape, lambda i: (0,) * len(shape))
    stress, part_w, part_e, part_s, part_n = pl.pallas_call(
        stress_kernel,
        grid=(elements // BLOCK,),
        in_specs=[
            whole(ROWS, nodes),
            pl.BlockSpec((CORNERS * COMPS, CORNERS * DOFS, BLOCK), lambda i: (0, 0, i)),
            pl.BlockSpec((CORNERS, BLOCK), lambda i: (0, i)),
        ],
        out_specs=[pl.BlockSpec((CORNERS * COMPS, MODES, BLOCK), lambda i: (0, 0, i))]
        + [whole(BORDER, WIDE)] * 4,
        out_shape=[
            jax.ShapeDtypeStruct((CORNERS * COMPS, MODES, elements), BF),
            side, side, side, side,
        ],
        scratch_shapes=[
            pltpu.VMEM((BLOCK // LANES, CORNERS * COMPS, CORNERS * DOFS, LANES), F32),
            pltpu.VMEM((BLOCK // LANES, CORNERS, ROWS, LANES), F32),
            pltpu.VMEM((TALL, LANES), F32),
        ],
        compiler_params=params(),
        cost_estimate=pl.CostEstimate(flops=10**10, bytes_accessed=10**7, transcendentals=0),
        name="stress",
    )(modes_disp, recovery, connect)
    got_w = ring(part_e, "px", 1)
    got_e = ring(part_w, "px", -1)
    got_s = ring(part_n, "py", 1)
    got_n = ring(part_s, "py", -1)
    big = BLOCK
    near, ids = pl.pallas_call(
        scatter_kernel,
        grid=(elements // big,),
        in_specs=[
            pl.BlockSpec((CORNERS * COMPS, MODES, big), lambda i: (0, 0, i)),
            pl.BlockSpec((CORNERS, big), lambda i: (0, i)),
            whole(CORNERS, elements),
            whole(1, reads),
            whole(CORNERS * COMPS, reads),
        ],
        out_specs=[whole(CORNERS, MODES + 8, reads), whole(CORNERS, reads)],
        out_shape=[
            jax.ShapeDtypeStruct((CORNERS, MODES + 8, reads), F32),
            jax.ShapeDtypeStruct((CORNERS, reads), jnp.int32),
        ],
        scratch_shapes=[
            pltpu.VMEM((tiles, TILE, LANES), jnp.int16),
            pltpu.VMEM((tiles, TALL, TILE), F32),
        ],
        compiler_params=params(),
        cost_estimate=pl.CostEstimate(flops=10**10, bytes_accessed=10**7, transcendentals=0),
        name="scatter",
    )(stress, connect, connect, read_elem.reshape(1, reads), read_wts)
    outgoing = pl.pallas_call(
        functools.partial(readout_kernel, zones=zones, cap=cap),
        in_specs=[full] * 8,
        out_specs=full,
        out_shape=jax.ShapeDtypeStruct((zones * cap, LANES), BF),
        compiler_params=params(),
        name="readout",
    )(near, ids, got_w, got_e, got_s, got_n, read_wts, zone.reshape(1, reads))
    arrived = lax.all_to_all(
        outgoing.reshape(zones, cap, LANES), ("px", "py"), split_axis=0, concat_axis=0, tiled=True
    ).reshape(zones * cap, LANES)
    deep = jnp.pad(response, ((0, LANES - MODES), (0, 0)))
    return jnp.dot(arrived, deep, preferred_element_type=F32).astype(BF)


def solution(mesh):
    placed = (
        P(None, ("px", "py")),
        P(None, None, ("px", "py")),
        P(None, ("px", "py")),
        P(("px", "py")),
        P(None, ("px", "py")),
        P(("px", "py"), None),
        P(),
    )
    return jax.shard_map(
        per_device, mesh=mesh, in_specs=placed, out_specs=P(("px", "py"), None), check_vma=False
    )
```
